32 devices in a mesh: row: 4 (over x, core), col: 8 (over z, y).
Axes of the slice: x: 2, y: 2, z: 4, core: 2. Of those that a mesh axis runs over, the one named last changes fastest.
Arguments:
- amp_ladder: bfloat16 [8, 16, 128, 16, 128], P('row', 'col'), may hold values from -6 to 6
- integrals: bfloat16 [8, 12, 128, 16, 128], P(None, 'row', None, 'col'), may hold values from -0.125 to 0.125
- residual_in: float32 [8, 12, 128, 16, 128], P(None, 'row', None, 'col'), may hold values from -6 to 6
Outputs:
- residual_out: float32 [8, 12, 128, 16, 128], P(None, 'row', None, 'col')
The draws below stay inside these ranges and needn't reach their ends.
All inputs are finite; a program needn't handle non-finite values.
Results may differ from the reference program's by a relative error of at most 0.0003.
Values may be sent and summed in bfloat16 or wider, within the bound.
No kernel may reach another device: no remote copies, remote signals or barrier semaphores. Data moves between devices by JAX's collectives and lax.ppermute only.
A program may use at most 192 MiB of HBM per device.

```python
import jax
import jax.numpy as jnp
from jax import lax

IRREPS = 8
BLK = 128
RPI = 12
KPI = 16
CPI = 16


def shard_levels(key, dims, split, low, high):
    def one(position, parts):
        steps = jax.random.uniform(jax.random.fold_in(jax.random.fold_in(key, 6), position), (parts,), jnp.float32, low / len(split), high / len(split))
        return jnp.repeat(jnp.exp(steps), dims[position] // parts).reshape((-1,) + (1,) * (len(dims) - position - 1))

    level = one(*split[0])
    for cut in split[1:]:
        level = level * one(*cut)
    return level


def scatter_about(own_key, extent, scale, bound, split=(), held_as=jnp.bfloat16):
    level = shard_levels(own_key, extent, split, -0.22, 0.18) if split else 1.0
    result = jax.random.normal(own_key, extent, jnp.float32) * scale * level
    return jnp.minimum(jnp.maximum(result, -bound), bound).astype(held_as)


def setup_inputs(seed: int = 0) -> dict:
    key_of = jax.random.split(jax.random.key(seed), 4)
    amp_ladder = scatter_about(key_of[0], (IRREPS, KPI, BLK, CPI, BLK), 1.0, 6.0, ((0, 4), (1, 8)))
    integrals = scatter_about(key_of[1], (IRREPS, RPI, BLK, KPI, BLK), (KPI * BLK) ** -0.5, 0.125, ((1, 4), (3, 8)))
    residual_in = scatter_about(key_of[2], (IRREPS, RPI, BLK, CPI, BLK), 1.0, 6.0, ((1, 4), (3, 8)), jnp.float32)
    return dict(amp_ladder=amp_ladder, integrals=integrals, residual_in=residual_in)


def irrep_cycle(pair):
    left, right = pair
    rows = left.shape[0] * left.shape[1]
    inner = left.shape[2] * left.shape[3]
    cols = right.shape[2] * right.shape[3]
    product = jnp.dot(left.astype(jnp.float32).reshape(rows, inner), right.astype(jnp.float32).reshape(inner, cols), precision=lax.Precision.HIGHEST, preferred_element_type=jnp.float32)
    return product.reshape(left.shape[0], left.shape[1], right.shape[2], right.shape[3])


def reference(amp_ladder, integrals, residual_in):
    cycle = lax.map(irrep_cycle, (integrals, amp_ladder))
    return residual_in + cycle
```

```python
import jax
import jax.numpy as jnp
from jax import lax
from jax.sharding import PartitionSpec as P

F32, F16 = jnp.float32, jnp.float16


def gathered(amp_ladder, integrals, residual_in):
    irreps, row_blocks, block = integrals.shape[:3]
    moved = lax.all_to_all(amp_ladder, "col", split_axis=3, concat_axis=1, tiled=True)
    right = lax.all_gather(moved, "row", axis=0, tiled=True)
    left = lax.all_gather(integrals, "col", axis=3, tiled=True)
    inner = left.shape[3] * block
    columns = right.shape[3]
    left = left.reshape(irreps, row_blocks * block, inner)
    right = right.reshape(irreps, inner, columns * block)
    cycle = jnp.einsum("hik,hkj->hij", left, right, preferred_element_type=F32)
    return residual_in + cycle.reshape(irreps, row_blocks, block, columns, block)


def along_z(pairs):
    return [(2 * a + y, 2 * b + y) for a, b in pairs for y in range(2)]


SWAP_Y = [(c, c ^ 1) for c in range(8)]
SWAP_CORE = [(r, r ^ 1) for r in range(4)]
SWAP_X = [(r, r ^ 2) for r in range(4)]
XOR_Z = {d: along_z([(z, z ^ d) for z in range(4)]) for d in (1, 2, 3)}
MIDDLE = along_z([(1, 2), (2, 1)])
INWARD = along_z([(0, 1), (3, 2)])
OUTWARD = along_z([(1, 0), (2, 3)])


def col(x, pairs):
    return lax.ppermute(x, "col", pairs)


def row(x, pairs):
    return lax.ppermute(x, "row", pairs)


def pick(x, i, axis=0):
    return lax.dynamic_index_in_dim(x, i, axis, keepdims=False)


def dot(a, b):
    return jnp.einsum("hik,hkj->hij", a, b, preferred_element_type=F32)


def over_row(piece):
    two = jnp.stack([piece, row(piece, SWAP_X)])
    return jnp.concatenate([two, row(two, SWAP_CORE)])


def mixed(amp_ladder, integrals, residual_in):
    irreps, row_blocks, block, k_blocks, _ = integrals.shape
    rows, kk = row_blocks * block, k_blocks * block
    r, c = lax.axis_index("row"), lax.axis_index("col")
    z, y = c // 2, c % 2
    order = [r, r ^ 2, r ^ 1, r ^ 3]
    middle = (z == 1) | (z == 2)

    left = integrals.reshape(irreps // 2, 2, rows, kk)
    left = [jnp.stack([pick(left[:, s], q) for q in order]) for s in range(2)]
    right = amp_ladder.reshape(2, kk, 4, 2, 2 * block)
    right = right.transpose(0, 2, 3, 1, 4)

    a_own, b0 = left[0], right[0]
    b_own, b_other = pick(b0, y, 1), pick(b0, 1 - y, 1)
    b_in = col(b_other, SWAP_Y)
    a_in = col(a_own, SWAP_Y)
    bo = over_row(b_own)
    bi = over_row(b_in)

    g, b1 = left[1], right[1]
    g1 = col(g, XOR_Z[1])
    gm3 = col(g, MIDDLE)
    gm2 = col(g1, MIDDLE)
    ge2 = col(gm3, OUTWARD)
    ge3 = col(gm2, OUTWARD)
    pieces = [pick(b1, z)] + [col(pick(b1, z ^ d), XOR_Z[d]) for d in (1, 2, 3)]
    near = over_row(jnp.stack(pieces[:2]))
    far = over_row(jnp.stack(pieces[2:]))

    def part(d):
        t = z ^ d
        return dot(a_own, pick(bo, t, 1)) + dot(a_in, pick(bi, t, 1))

    p3, p2, p1, p0 = part(3), part(2), part(1), part(0)
    s1 = col(p3.astype(F16), INWARD)
    send = (p2 + s1.astype(F32)).astype(F16)
    s2a = col(send, INWARD)
    s2b = col(send, MIDDLE)
    s3a = col((p1 + s2b.astype(F32)).astype(F16), XOR_Z[1])
    s3b = col((p3 + s2a.astype(F32)).astype(F16), MIDDLE)
    even = p0 + s3a.astype(F32) + s3b.astype(F32)

    g2 = jnp.where(middle, gm2, ge2)
    g3 = jnp.where(middle, gm3, ge3)

    def column(which):
        take = lambda b, i: pick(b[:, i], which, 1)
        return (dot(g, take(near, 0)) + dot(g1, take(near, 1))) + (dot(g2, take(far, 0)) + dot(g3, take(far, 1)))

    q = col(column(1 - y).astype(F16), SWAP_Y)
    odd = column(y) + q.astype(F32)

    both = jnp.stack([even, odd], 1)
    back = []
    for q in range(irreps // 2):
        m = r ^ q
        back.append(pick(both, (m >> 1) | ((m & 1) << 1)))
    cycle = jnp.concatenate(back).reshape(residual_in.shape)
    return residual_in + cycle


def solution(mesh):
    placed = (
        P("row", "col", None, None, None),
        P(None, "row", None, "col", None),
        P(None, "row", None, "col", None),
    )

    def per_device(amp_ladder, integrals, residual_in):
        fits = mesh.shape["row"] == 4 and mesh.shape["col"] == 8
        fits = fits and amp_ladder.shape[0] == 2 and residual_in.shape[3] == 2 and amp_ladder.shape[1] == 2
        return (mixed if fits else gathered)(amp_ladder, integrals, residual_in)

    return jax.shard_map(
        per_device,
        mesh=mesh,
        in_specs=placed,
        out_specs=P(None, "row", None, "col", None),
        check_vma=False,
    )
```

```python
import jax
import jax.numpy as jnp
from jax import lax
from jax.experimental import pallas as pl
from jax.experimental.pallas import tpu as pltpu
from jax.sharding import PartitionSpec as P

BF16, F16, F32 = jnp.bfloat16, jnp.float16, jnp.float32
PARAMS = pltpu.CompilerParams(vmem_limit_bytes=32 * 2**20)


def gathered(amp_ladder, integrals, residual_in):
    irreps, row_blocks, block = integrals.shape[:3]
    moved = lax.all_to_all(amp_ladder, "col", split_axis=3, concat_axis=1, tiled=True)
    right = lax.all_gather(moved, "row", axis=0, tiled=True)
    left = lax.all_gather(integrals, "col", axis=3, tiled=True)
    inner = left.shape[3] * block
    columns = right.shape[3]
    left = left.reshape(irreps, row_blocks * block, inner)
    right = right.reshape(irreps, inner, columns * block)
    cycle = jnp.einsum("hik,hkj->hij", left, right, preferred_element_type=F32)
    return residual_in + cycle.reshape(irreps, row_blocks, block, columns, block)


def along_z(pairs):
    return [(2 * a + y, 2 * b + y) for a, b in pairs for y in range(2)]


SWAP_Y = [(c, c ^ 1) for c in range(8)]
SWAP_CORE = [(r, r ^ 1) for r in range(4)]
SWAP_X = [(r, r ^ 2) for r in range(4)]
XOR_Z = {d: along_z([(z, z ^ d) for z in range(4)]) for d in (1, 2, 3)}
MIDDLE = along_z([(1, 2), (2, 1)])
INWARD = along_z([(0, 1), (3, 2)])
OUTWARD = along_z([(1, 0), (2, 3)])


def col(x, pairs):
    return lax.ppermute(x, "col", pairs)


def row(x, pairs):
    return lax.ppermute(x, "row", pairs)


def after(x, *others):
    return lax.optimization_barrier((x, *others))[0]


def call(body, place, grid, ins, outs, shapes, operands, scratch=(), flops=0, **more):
    given = sum(o.size * o.dtype.itemsize for o in operands)
    made = sum(o.size * o.dtype.itemsize for o in jax.tree.leaves(shapes))
    return pl.pallas_call(
        body,
        grid_spec=pltpu.PrefetchScalarGridSpec(
            num_scalar_prefetch=1, grid=grid, in_specs=ins, out_specs=outs, scratch_shapes=list(scratch)
        ),
        out_shape=shapes,
        compiler_params=PARAMS,
        cost_estimate=pl.CostEstimate(flops=flops, bytes_accessed=given + made, transcendentals=0),
        **more,
    )(place, *operands)


def split_rows(place, pairs):
    irreps, double, lanes = pairs.shape
    rows = double // 2

    def body(_, in_ref, even_ref, odd_ref, wide):
        for n, out in enumerate((even_ref, odd_ref)):
            wide[...] = in_ref[n].astype(F32)
            for b in range(2):
                out[0, :, b * lanes : (b + 1) * lanes] = wide[pl.ds(b, rows, stride=2), :].astype(BF16)

    shape = jax.ShapeDtypeStruct((irreps // 2, rows, 2 * lanes), BF16)
    spec = pl.BlockSpec((1, rows, 2 * lanes), lambda i, _: (i, 0, 0))
    return call(
        body, place, (irreps // 2,),
        [pl.BlockSpec((2, double, lanes), lambda i, _: (i, 0, 0))],
        [spec, spec], [shape, shape], [pairs], [pltpu.VMEM((double, lanes), F32)],
    )


def pick_columns(place, amps, irrep, tables):
    _, k_blocks, block, columns, lanes = amps.shape
    sizes = [len(t) for t in tables([0, 0, 0])]

    def body(place_ref, in_ref, *refs):
        outs, wide = refs[:-1], refs[-1]
        wide[...] = in_ref[0, 0].astype(F32).reshape(wide.shape)
        for out, table in zip(outs, tables(place_ref)):
            for n, pair in enumerate(table):
                for b, j in enumerate(pair):
                    out[n, :, b * lanes : (b + 1) * lanes] = wide[pl.ds(j, block, stride=columns), :].astype(BF16)

    return call(
        body, place, (k_blocks,),
        [pl.BlockSpec((1, 1, block, columns, lanes), lambda k, _: (irrep, k, 0, 0, 0))],
        [pl.BlockSpec((n, block, 2 * lanes), lambda k, _: (0, k, 0)) for n in sizes],
        [jax.ShapeDtypeStruct((n, k_blocks * block, 2 * lanes), BF16) for n in sizes],
        [amps], [pltpu.VMEM((block * columns, lanes), F32)],
    )


def across(m):
    return (0, 2, 1, 3)[m]


def parts(place, lefts, rights, steps):
    irreps, rows, kk = lefts[0].shape
    wide = rights[0][0].shape[-1]
    flat = [b for source in rights for b in source]

    def body(place_ref, *refs):
        a_refs, refs = refs[: len(lefts)], refs[len(lefts) :]
        b_refs, outs = refs[: len(flat) * len(steps)], refs[len(flat) * len(steps) :]
        for m in range(4):

            @pl.when(pl.program_id(0) == m)
            def _():
                for n, out in enumerate(outs):
                    total = None
                    for s, a in enumerate(a_refs):
                        b = b_refs[n * len(flat) + 4 * s + m]
                        term = jnp.dot(a[0], b[0], preferred_element_type=F32)
                        total = term if total is None else total + term
                    out[0] = total

    irrep_of = lambda m, p: (p[0] ^ (((m & 1) << 1) | (m >> 1)), 0, 0)
    return call(
        body, place, (irreps,),
        [pl.BlockSpec((1, rows, kk), irrep_of)] * len(lefts)
        + [pl.BlockSpec((1, kk, wide), lambda m, p, d=d: (p[1] ^ d, 0, 0)) for d in steps for _ in flat],
        [pl.BlockSpec((1, rows, wide), irrep_of)] * len(steps),
        [jax.ShapeDtypeStruct((irreps, rows, wide), F32)] * len(steps),
        [*lefts, *(flat * len(steps))],
        flops=2 * irreps * rows * kk * wide * len(lefts) * len(steps),
    )


def column(place, lefts, pairs, other):
    irreps, rows, kk = lefts[0].shape
    wide = pairs[0][0].shape[-1]
    flat = [b for pair in pairs for b in pair]

    def body(place_ref, *refs):
        a_refs, b_refs, out = refs[:4], refs[4:-1], refs[-1]
        for m in range(4):

            @pl.when(pl.program_id(0) == m)
            def _():
                total = None
                for s, a in enumerate(a_refs):
                    b = b_refs[4 * (s // 2) + m]
                    term = jnp.dot(a[0], b[s % 2, 0], preferred_element_type=F32)
                    total = term if total is None else total + term
                out[0] = total

    irrep_of = lambda m, p: (p[0] ^ (((m & 1) << 1) | (m >> 1)), 0, 0)
    return call(
        body, place, (irreps,),
        [pl.BlockSpec((1, rows, kk), irrep_of)] * 4
        + [pl.BlockSpec((2, 1, kk, wide), lambda m, p: (0, p[2] ^ other, 0, 0))] * len(flat),
        pl.BlockSpec((1, rows, wide), irrep_of),
        jax.ShapeDtypeStruct((irreps, rows, wide), F32),
        [*lefts, *flat],
        flops=2 * irreps * rows * kk * wide * 4,
    )


def add_half(place, residual, cycle, parity, result=None):
    irreps, double, lanes = residual.shape
    rows = double // 2

    def body(_, res_ref, add_ref, *refs):
        out = refs[-1]
        for b in range(2):
            place = pl.ds(b, rows, stride=2)
            out[0, place, :] = res_ref[0, place, :] + add_ref[0, :, b * lanes : (b + 1) * lanes]

    mine = pl.BlockSpec((1, double, lanes), lambda i, _: (2 * i + parity, 0, 0))
    given = [] if result is None else [result]
    return call(
        body, place, (irreps // 2,),
        [mine, pl.BlockSpec((1, rows, 2 * lanes), lambda i, _: (i, 0, 0))] + [pl.BlockSpec(memory_space=pl.ANY)] * len(given),
        mine,
        jax.ShapeDtypeStruct(residual.shape, F32),
        [residual, cycle, *given],
        input_output_aliases={3: 0} if given else {},
    )


def mixed(amp_ladder, integrals, residual_in):
    irreps, row_blocks, block, k_blocks, _ = integrals.shape
    r, c = lax.axis_index("row"), lax.axis_index("col")
    z, y = c // 2, c % 2
    middle = (z == 1) | (z == 2)
    place = jnp.stack([r, z, y]).astype(jnp.int32)

    tables = lambda p: [[[4 * t + 2 * w + b for b in range(2)] for t in range(4)] for w in (p[2], 1 - p[2])]
    b_own, b_other = pick_columns(place, amp_ladder, 0, tables)
    a_even, g = split_rows(place, integrals.reshape(irreps, row_blocks * block * k_blocks, block))
    tables = lambda p: [[[4 * (p[1] ^ d) + 2 * w + b for b in range(2)] for w in range(2)] for d in range(4)]
    pieces = pick_columns(place, amp_ladder, 1, tables)

    hold = lax.optimization_barrier
    core = lambda a, b: [a, b, row(a, SWAP_CORE), row(b, SWAP_CORE)]

    g1 = col(g, XOR_Z[1])
    g3_mid = col(g, MIDDLE)
    b_in = col(b_other, SWAP_Y)
    x_own = row(b_own, SWAP_X)

    b_in, *pieces = hold((b_in, *pieces))
    got = [col(pieces[d], XOR_Z[d]) for d in (1, 2, 3)]
    a_in = col(after(a_even, b_in), SWAP_Y)
    x_in = row(b_in, SWAP_X)

    g1, g3_mid, x_own, x_in = hold((g1, g3_mid, x_own, x_in))
    g2_mid = col(g1, MIDDLE)
    g2_end = col(g3_mid, OUTWARD)
    b_rows = [core(b_own, x_own), core(b_in, x_in)]
    a_in, got, b_rows = hold((a_in, got, b_rows))

    (p3,) = parts(place, [a_even, a_in], b_rows, [3])
    i3 = col(p3.astype(F16), INWARD)
    near = jnp.stack([pieces[0], got[0]])
    near = core(near, row(after(near, p3), SWAP_X))
    p2, p1, p0 = parts(place, [after(a_even, p3), a_in], b_rows, [2, 1, 0])

    i3, g2_mid, g2_end, p2, near = hold((i3, g2_mid, g2_end, p2, near))
    i2 = col(p2.astype(F16), INWARD)
    m2 = col((p2 + i3.astype(F32)).astype(F16), MIDDLE)
    g3_end = col(g2_mid, OUTWARD)
    far = jnp.stack([got[1], got[2]])
    far = core(far, row(after(far, near[0]), SWAP_X))

    i2, m2, g3_end, far, p3 = hold((i2, m2, g3_end, far, p3))
    s1 = col((p1 + m2.astype(F32)).astype(F16), XOR_Z[1])
    m3 = col((p3 + i2.astype(F32)).astype(F16), MIDDLE)
    lefts = [g, g1, jnp.where(middle, g2_mid, g2_end), jnp.where(middle, g3_mid, g3_end)]
    q = col(column(place, lefts, [near, far], 1).astype(F16), SWAP_Y)
    even = (p0 + s1.astype(F32)) + m3.astype(F32)
    odd = column(place, lefts, [near, far], 0) + q.astype(F32)

    result = residual_in.reshape(irreps, row_blocks * block * 2, block)
    done = add_half(place, result, odd, 1)
    done = add_half(place, result, even, 0, done)
    return done.reshape(residual_in.shape)


def solution(mesh):
    placed = (
        P("row", "col", None, None, None),
        P(None, "row", None, "col", None),
        P(None, "row", None, "col", None),
    )

    def per_device(amp_ladder, integrals, residual_in):
        fits = mesh.shape["row"] == 4 and mesh.shape["col"] == 8
        fits = fits and amp_ladder.shape[0] == 2 and residual_in.shape[3] == 2 and amp_ladder.shape[1] == 2
        return (mixed if fits else gathered)(amp_ladder, integrals, residual_in)

    return jax.shard_map(
        per_device,
        mesh=mesh,
        in_specs=placed,
        out_specs=P(None, "row", None, "col", None),
        check_vma=False,
    )
```

```python
import jax
import jax.numpy as jnp
from jax import lax
from jax.experimental import pallas as pl
from jax.experimental.pallas import tpu as pltpu
from jax.sharding import PartitionSpec as P

BF16, F16, F32 = jnp.bfloat16, jnp.float16, jnp.float32
WIRE = 32.0
LONG = 48 * 2**20
PARAMS = pltpu.CompilerParams(vmem_limit_bytes=32 * 2**20)


def gathered(amp_ladder, integrals, residual_in):
    irreps, row_blocks, block = integrals.shape[:3]
    moved = lax.all_to_all(amp_ladder, "col", split_axis=3, concat_axis=1, tiled=True)
    right = lax.all_gather(moved, "row", axis=0, tiled=True)
    left = lax.all_gather(integrals, "col", axis=3, tiled=True)
    inner = left.shape[3] * block
    columns = right.shape[3]
    left = left.reshape(irreps, row_blocks * block, inner)
    right = right.reshape(irreps, inner, columns * block)
    cycle = jnp.einsum("hik,hkj->hij", left, right, preferred_element_type=F32)
    return residual_in + cycle.reshape(irreps, row_blocks, block, columns, block)


def along_z(pairs):
    return [(2 * a + y, 2 * b + y) for a, b in pairs for y in range(2)]


SWAP_Y = [(c, c ^ 1) for c in range(8)]
SWAP_CORE = [(r, r ^ 1) for r in range(4)]
SWAP_X = [(r, r ^ 2) for r in range(4)]
XOR_Z = {d: along_z([(z, z ^ d) for z in range(4)]) for d in (1, 2, 3)}
MIDDLE = along_z([(1, 2), (2, 1)])
INWARD = along_z([(0, 1), (3, 2)])
OUTWARD = along_z([(1, 0), (2, 3)])


def col(x, pairs):
    return lax.ppermute(x, "col", pairs)


def row(x, pairs):
    return lax.ppermute(x, "row", pairs)


def to_wire(x, pairs):
    return col((x * WIRE).astype(F16), pairs)


def from_wire(x):
    return x.astype(F32) * (1 / WIRE)


def after(x, *others):
    return lax.optimization_barrier((x, *others))[0]


def call(body, place, grid, ins, outs, shapes, operands, scratch=(), cost=0, **more):
    return pl.pallas_call(
        body,
        grid_spec=pltpu.PrefetchScalarGridSpec(
            num_scalar_prefetch=1, grid=grid, in_specs=ins, out_specs=outs, scratch_shapes=list(scratch)
        ),
        out_shape=shapes,
        compiler_params=PARAMS,
        cost_estimate=pl.CostEstimate(flops=0, bytes_accessed=cost, transcendentals=0),
        **more,
    )(place, *operands)


def split_rows(place, pairs):
    irreps, double, lanes = pairs.shape
    rows = double // 2

    def body(_, in_ref, even_ref, odd_ref, wide):
        for n, out in enumerate((even_ref, odd_ref)):
            wide[...] = in_ref[n].astype(F32)
            for b in range(2):
                out[0, :, b * lanes : (b + 1) * lanes] = wide[pl.ds(b, rows, stride=2), :].astype(BF16)

    shape = jax.ShapeDtypeStruct((irreps // 2, rows, 2 * lanes), BF16)
    spec = pl.BlockSpec((1, rows, 2 * lanes), lambda i, _: (i, 0, 0))
    return call(
        body, place, (irreps // 2,),
        [pl.BlockSpec((2, double, lanes), lambda i, _: (i, 0, 0))],
        [spec, spec], [shape, shape], [pairs], [pltpu.VMEM((double, lanes), F32)],
    )


def pick_columns(place, amps, irrep, tables):
    _, k_blocks, block, columns, lanes = amps.shape
    sizes = [len(t) for t in tables([0, 0, 0])]

    def body(place_ref, in_ref, *refs):
        outs, wide = refs[:-1], refs[-1]
        wide[...] = in_ref[0, 0].astype(F32).reshape(wide.shape)
        for out, table in zip(outs, tables(place_ref)):
            for n, pair in enumerate(table):
                for b, j in enumerate(pair):
                    out[n, :, b * lanes : (b + 1) * lanes] = wide[pl.ds(j, block, stride=columns), :].astype(BF16)

    return call(
        body, place, (k_blocks,),
        [pl.BlockSpec((1, 1, block, columns, lanes), lambda k, _: (irrep, k, 0, 0, 0))],
        [pl.BlockSpec((n, block, 2 * lanes), lambda k, _: (0, k, 0)) for n in sizes],
        [jax.ShapeDtypeStruct((n, k_blocks * block, 2 * lanes), BF16) for n in sizes],
        [amps], [pltpu.VMEM((block * columns, lanes), F32)],
    )


def across(m):
    return (0, 2, 1, 3)[m]


def parts(place, lefts, rights, steps, cost=0):
    irreps, rows, kk = lefts[0].shape
    wide = rights[0][0].shape[-1]
    flat = [b for source in rights for b in source]

    def body(place_ref, *refs):
        a_refs, refs = refs[: len(lefts)], refs[len(lefts) :]
        b_refs, outs = refs[: len(flat) * len(steps)], refs[len(flat) * len(steps) :]
        for m in range(4):

            @pl.when(pl.program_id(0) == m)
            def _():
                for n, out in enumerate(outs):
                    total = None
                    for s, a in enumerate(a_refs):
                        b = b_refs[n * len(flat) + 4 * s + m]
                        term = jnp.dot(a[0], b[0], preferred_element_type=F32)
                        total = term if total is None else total + term
                    out[0] = total

    irrep_of = lambda m, p: (p[0] ^ (((m & 1) << 1) | (m >> 1)), 0, 0)
    return call(
        body, place, (irreps,),
        [pl.BlockSpec((1, rows, kk), irrep_of)] * len(lefts)
        + [pl.BlockSpec((1, kk, wide), lambda m, p, d=d: (p[1] ^ d, 0, 0)) for d in steps for _ in flat],
        [pl.BlockSpec((1, rows, wide), irrep_of)] * len(steps),
        [jax.ShapeDtypeStruct((irreps, rows, wide), F32)] * len(steps),
        [*lefts, *(flat * len(steps))],
        cost=cost,
    )


def column(place, terms, other, cost, start=None):
    irreps, rows, kk = terms[0][0].shape
    wide = terms[0][1][0].shape[-1]
    lefts = [t[0] for t in terms]
    flat = [b for t in terms for b in t[1]]
    given = [] if start is None else [start]

    def body(place_ref, *refs):
        a_refs, b_refs, out = refs[: len(terms)], refs[len(terms) : 5 * len(terms)], refs[-1]
        for m in range(4):

            @pl.when(pl.program_id(0) == m)
            def _():
                total = refs[-2][0] if given else None
                for s, a in enumerate(a_refs):
                    term = jnp.dot(a[0], b_refs[4 * s + m][0, 0], preferred_element_type=F32)
                    total = term if total is None else total + term
                out[0] = total

    irrep_of = lambda m, p: (p[0] ^ (((m & 1) << 1) | (m >> 1)), 0, 0)
    sums = pl.BlockSpec((1, rows, wide), irrep_of)
    return call(
        body, place, (irreps,),
        [pl.BlockSpec((1, rows, kk), irrep_of)] * len(terms)
        + [pl.BlockSpec((1, 1, kk, wide), lambda m, p, n=t[2]: (n, p[2] ^ other, 0, 0)) for t in terms for _ in range(4)]
        + [sums] * len(given),
        sums,
        jax.ShapeDtypeStruct((irreps, rows, wide), F32),
        [*lefts, *flat, *given],
        cost=cost,
    )


def stretch(place, cost):
    def body(in_ref, out_ref):
        for n in range(place.shape[0]):
            out_ref[n] = in_ref[n]

    return pl.pallas_call(
        body,
        in_specs=[pl.BlockSpec(memory_space=pltpu.SMEM)],
        out_specs=pl.BlockSpec(memory_space=pltpu.SMEM),
        out_shape=jax.ShapeDtypeStruct(place.shape, place.dtype),
        cost_estimate=pl.CostEstimate(flops=0, bytes_accessed=cost, transcendentals=0),
    )(place)


def add_all(place, residual, even, odd):
    irreps, double, lanes = residual.shape
    rows = double // 2

    def body(_, res_ref, even_ref, odd_ref, out):
        for n, add_ref in enumerate((even_ref, odd_ref)):
            for b in range(2):
                spot = pl.ds(b, rows, stride=2)
                out[n, spot, :] = res_ref[n, spot, :] + add_ref[0, :, b * lanes : (b + 1) * lanes]

    pair = pl.BlockSpec((2, double, lanes), lambda i, _: (i, 0, 0))
    half = pl.BlockSpec((1, rows, 2 * lanes), lambda i, _: (i, 0, 0))
    return call(
        body, place, (irreps // 2,), [pair, half, half], pair,
        jax.ShapeDtypeStruct(residual.shape, F32), [residual, even, odd],
    )


def mixed(amp_ladder, integrals, residual_in):
    irreps, row_blocks, block, k_blocks, _ = integrals.shape
    r, c = lax.axis_index("row"), lax.axis_index("col")
    z, y = c // 2, c % 2
    middle = (z == 1) | (z == 2)
    place = jnp.stack([r, z, y]).astype(jnp.int32)

    a_even, g = split_rows(place, integrals.reshape(irreps, row_blocks * block * k_blocks, block))
    amp_ladder = after(amp_ladder, g)
    tables = lambda p: [[[4 * t + 2 * w + b for b in range(2)] for t in range(4)] for w in (p[2], 1 - p[2])]
    b_own, b_other = pick_columns(place, amp_ladder, 0, tables)
    tables = lambda p: [[[4 * (p[1] ^ d) + 2 * w + b for b in range(2)] for w in range(2)] for d in range(4)]
    pieces = pick_columns(place, amp_ladder, 1, tables)

    hold = lax.optimization_barrier

    g1 = col(g, XOR_Z[1])
    b_in = col(b_other, SWAP_Y)
    x_own = row(b_own, SWAP_X)
    g3_mid = col(after(g, b_other), MIDDLE)
    pieces, g1, g3_mid, x_own, b_in, b_own = hold((pieces, g1, g3_mid, x_own, b_in, b_own))

    x_in = row(b_in, SWAP_X)
    a_in = col(after(a_even, b_in), SWAP_Y)
    swapped = [row(b, SWAP_CORE) for b in (b_own, x_own, b_in)]
    pieces, swapped = hold((pieces, swapped))
    got = [col(pieces[d], XOR_Z[d]) for d in (3, 2, 1)]
    x_in, got = hold((x_in, got))

    swapped.append(row(x_in, SWAP_CORE))
    a_in, got, swapped = hold((a_in, got, swapped))
    b_rows = [[b_own, x_own, swapped[0], swapped[1]], [b_in, x_in, swapped[2], swapped[3]]]

    (p3,) = parts(place, [a_even, a_in], b_rows, [3])
    wire3 = (p3 * WIRE).astype(F16)

    wire3, g1, g3_mid, got = hold((wire3, g1, g3_mid, got))
    got = jnp.stack([pieces[0], got[2], got[1], got[0]])
    i3 = col(wire3, INWARD)
    g2_end = col(g3_mid, OUTWARD)
    g2_mid = col(g1, MIDDLE)
    got_x = row(got, SWAP_X)
    p2, p1, p0 = parts(place, [after(a_even, wire3), a_in], b_rows, [2, 1, 0])
    wire2 = (p2 * WIRE).astype(F16)
    i2 = col(wire2, INWARD)
    turn2 = ((p2 + from_wire(i3)) * WIRE).astype(F16)
    turn2, p1, g2_mid, got_x, g2_end = hold((turn2, p1, g2_mid, got_x, g2_end))


    m2 = col(turn2, MIDDLE)
    g3_end = col(g2_mid, OUTWARD)
    got_rows = [got, got_x, row(got, SWAP_CORE), row(got_x, SWAP_CORE)]

    lefts = [g, g1, jnp.where(middle, g2_mid, g2_end), jnp.where(middle, g3_mid, g3_end)]
    terms = [(left, got_rows, n) for n, left in enumerate(lefts)]
    other = (column(place, terms, 1, 0) * WIRE).astype(F16)
    turn3 = ((p3 + from_wire(i2)) * WIRE).astype(F16)
    turn3, m2, other = hold((turn3, m2, other))

    q = col(other, SWAP_Y)
    s1 = to_wire(p1 + from_wire(m2), XOR_Z[1])
    m3 = col(turn3, MIDDLE)
    odd = column(place, terms, 0, 0) + from_wire(q)
    even, m3, odd = hold((p0 + from_wire(s1), m3, odd))
    even = even + from_wire(m3)

    result = residual_in.reshape(irreps, row_blocks * block * 2, block)
    done = add_all(place, result, even, odd)
    return done.reshape(residual_in.shape)


def solution(mesh):
    placed = (
        P("row", "col", None, None, None),
        P(None, "row", None, "col", None),
        P(None, "row", None, "col", None),
    )

    def per_device(amp_ladder, integrals, residual_in):
        fits = mesh.shape["row"] == 4 and mesh.shape["col"] == 8
        fits = fits and amp_ladder.shape[0] == 2 and residual_in.shape[3] == 2 and amp_ladder.shape[1] == 2
        return (mixed if fits else gathered)(amp_ladder, integrals, residual_in)

    return jax.shard_map(
        per_device,
        mesh=mesh,
        in_specs=placed,
        out_specs=P(None, "row", None, "col", None),
        check_vma=False,
    )
```

```python
import jax
import jax.numpy as jnp
from jax import lax
from jax.experimental import pallas as pl
from jax.experimental.pallas import tpu as pltpu
from jax.sharding import PartitionSpec as P

BF16, F16, F32 = jnp.bfloat16, jnp.float16, jnp.float32
WIRE = 32.0
LONG = 48 * 2**20
PARAMS = pltpu.CompilerParams(vmem_limit_bytes=32 * 2**20)


def gathered(amp_ladder, integrals, residual_in):
    irreps, row_blocks, block = integrals.shape[:3]
    moved = lax.all_to_all(amp_ladder, "col", split_axis=3, concat_axis=1, tiled=True)
    right = lax.all_gather(moved, "row", axis=0, tiled=True)
    left = lax.all_gather(integrals, "col", axis=3, tiled=True)
    inner = left.shape[3] * block
    columns = right.shape[3]
    left = left.reshape(irreps, row_blocks * block, inner)
    right = right.reshape(irreps, inner, columns * block)
    cycle = jnp.einsum("hik,hkj->hij", left, right, preferred_element_type=F32)
    return residual_in + cycle.reshape(irreps, row_blocks, block, columns, block)


def along_z(pairs):
    return [(2 * a + y, 2 * b + y) for a, b in pairs for y in range(2)]


SWAP_Y = [(c, c ^ 1) for c in range(8)]
SWAP_CORE = [(r, r ^ 1) for r in range(4)]
SWAP_X = [(r, r ^ 2) for r in range(4)]
XOR_Z = {d: along_z([(z, z ^ d) for z in range(4)]) for d in (1, 2, 3)}
MIDDLE = along_z([(1, 2), (2, 1)])
INWARD = along_z([(0, 1), (3, 2)])
OUTWARD = along_z([(1, 0), (2, 3)])


def col(x, pairs):
    return lax.ppermute(x, "col", pairs)


def row(x, pairs):
    return lax.ppermute(x, "row", pairs)


def to_wire(x, pairs):
    return col((x * WIRE).astype(F16), pairs)


def from_wire(x):
    return x.astype(F32) * (1 / WIRE)


def after(x, *others):
    return lax.optimization_barrier((x, *others))[0]


def call(body, place, grid, ins, outs, shapes, operands, scratch=(), cost=0, **more):
    return pl.pallas_call(
        body,
        grid_spec=pltpu.PrefetchScalarGridSpec(
            num_scalar_prefetch=1, grid=grid, in_specs=ins, out_specs=outs, scratch_shapes=list(scratch)
        ),
        out_shape=shapes,
        compiler_params=PARAMS,
        cost_estimate=pl.CostEstimate(flops=0, bytes_accessed=cost, transcendentals=0),
        **more,
    )(place, *operands)


def split_rows(place, pairs):
    irreps, double, lanes = pairs.shape
    rows = double // 2

    def body(_, in_ref, even_ref, odd_ref, wide):
        for n, out in enumerate((even_ref, odd_ref)):
            wide[...] = in_ref[n].astype(F32)
            for b in range(2):
                out[0, :, b * lanes : (b + 1) * lanes] = wide[pl.ds(b, rows, stride=2), :].astype(BF16)

    shape = jax.ShapeDtypeStruct((irreps // 2, rows, 2 * lanes), BF16)
    spec = pl.BlockSpec((1, rows, 2 * lanes), lambda i, _: (i, 0, 0))
    return call(
        body, place, (irreps // 2,),
        [pl.BlockSpec((2, double, lanes), lambda i, _: (i, 0, 0))],
        [spec, spec], [shape, shape], [pairs], [pltpu.VMEM((double, lanes), F32)],
    )


def pick_columns(place, amps, irrep, tables):
    _, k_blocks, block, columns, lanes = amps.shape
    sizes = [len(t) for t in tables([0, 0, 0])]

    def body(place_ref, in_ref, *refs):
        outs, wide = refs[:-1], refs[-1]
        wide[...] = in_ref[0, 0].astype(F32).reshape(wide.shape)
        for out, table in zip(outs, tables(place_ref)):
            for n, pair in enumerate(table):
                for b, j in enumerate(pair):
                    out[n, :, b * lanes : (b + 1) * lanes] = wide[pl.ds(j, block, stride=columns), :].astype(BF16)

    return call(
        body, place, (k_blocks,),
        [pl.BlockSpec((1, 1, block, columns, lanes), lambda k, _: (irrep, k, 0, 0, 0))],
        [pl.BlockSpec((n, block, 2 * lanes), lambda k, _: (0, k, 0)) for n in sizes],
        [jax.ShapeDtypeStruct((n, k_blocks * block, 2 * lanes), BF16) for n in sizes],
        [amps], [pltpu.VMEM((block * columns, lanes), F32)],
    )


def across(m):
    return (0, 2, 1, 3)[m]


def parts(place, lefts, rights, steps, cost=0):
    irreps, rows, kk = lefts[0].shape
    wide = rights[0][0].shape[-1]
    flat = [b for source in rights for b in source]

    def body(place_ref, *refs):
        a_refs, refs = refs[: len(lefts)], refs[len(lefts) :]
        b_refs, outs = refs[: len(flat) * len(steps)], refs[len(flat) * len(steps) :]
        for m in range(4):

            @pl.when(pl.program_id(0) == m)
            def _():
                for n, out in enumerate(outs):
                    total = None
                    for s, a in enumerate(a_refs):
                        b = b_refs[n * len(flat) + 4 * s + m]
                        term = jnp.dot(a[0], b[0], preferred_element_type=F32)
                        total = term if total is None else total + term
                    out[0] = total

    irrep_of = lambda m, p: (p[0] ^ (((m & 1) << 1) | (m >> 1)), 0, 0)
    return call(
        body, place, (irreps,),
        [pl.BlockSpec((1, rows, kk), irrep_of)] * len(lefts)
        + [pl.BlockSpec((1, kk, wide), lambda m, p, d=d: (p[1] ^ d, 0, 0)) for d in steps for _ in flat],
        [pl.BlockSpec((1, rows, wide), irrep_of)] * len(steps),
        [jax.ShapeDtypeStruct((irreps, rows, wide), F32)] * len(steps),
        [*lefts, *(flat * len(steps))],
        cost=cost,
    )


def column(place, terms, other, start=None):
    irreps, rows, kk = terms[0][0][0].shape
    wide = terms[0][1][0].shape[-1]
    lefts = [left for t in terms for left in t[0]]
    flat = [b for t in terms for b in t[1]]
    given = [] if start is None else [start]

    def body(place_ref, *refs):
        a_refs, b_refs, out = refs[: len(lefts)], refs[len(lefts) : len(lefts) + len(flat)], refs[-1]
        for m in range(4):

            @pl.when(pl.program_id(0) == m)
            def _():
                total = refs[-2][0] if given else None
                at = 0
                for s, t in enumerate(terms):
                    left = a_refs[at][0]
                    if len(t[0]) == 2:
                        left = left + a_refs[at + 1][0]
                    at += len(t[0])
                    term = jnp.dot(left, b_refs[4 * s + m][0, 0], preferred_element_type=F32)
                    total = term if total is None else total + term
                out[0] = total

    irrep_of = lambda m, p: (p[0] ^ (((m & 1) << 1) | (m >> 1)), 0, 0)
    sums = pl.BlockSpec((1, rows, wide), irrep_of)
    return call(
        body, place, (irreps,),
        [pl.BlockSpec((1, rows, kk), irrep_of)] * len(lefts)
        + [pl.BlockSpec((1, 1, kk, wide), lambda m, p, n=t[2]: (n, p[2] ^ other, 0, 0)) for t in terms for _ in range(4)]
        + [sums] * len(given),
        sums,
        jax.ShapeDtypeStruct((irreps, rows, wide), F32),
        [*lefts, *flat, *given],
    )


def add_all(place, residual, even, odd):
    irreps, double, lanes = residual.shape
    rows = double // 2

    def body(_, res_ref, even_ref, odd_ref, out):
        for n, add_ref in enumerate((even_ref, odd_ref)):
            for b in range(2):
                spot = pl.ds(b, rows, stride=2)
                out[n, spot, :] = res_ref[n, spot, :] + add_ref[0, :, b * lanes : (b + 1) * lanes]

    pair = pl.BlockSpec((2, double, lanes), lambda i, _: (i, 0, 0))
    half = pl.BlockSpec((1, rows, 2 * lanes), lambda i, _: (i, 0, 0))
    return call(
        body, place, (irreps // 2,), [pair, half, half], pair,
        jax.ShapeDtypeStruct(residual.shape, F32), [residual, even, odd],
    )


def mixed(amp_ladder, integrals, residual_in):
    irreps, row_blocks, block, k_blocks, _ = integrals.shape
    r, c = lax.axis_index("row"), lax.axis_index("col")
    z, y = c // 2, c % 2
    middle = (z == 1) | (z == 2)
    place = jnp.stack([r, z, y]).astype(jnp.int32)

    a_even, g = split_rows(place, integrals.reshape(irreps, row_blocks * block * k_blocks, block))
    amp_ladder = after(amp_ladder, g)
    tables = lambda p: [[[4 * t + 2 * w + b for b in range(2)] for t in range(4)] for w in (p[2], 1 - p[2])]
    b_own, b_other = pick_columns(place, amp_ladder, 0, tables)
    tables = lambda p: [[[4 * (p[1] ^ d) + 2 * w + b for b in range(2)] for w in range(2)] for d in range(4)]
    pieces = pick_columns(place, amp_ladder, 1, tables)

    hold = lax.optimization_barrier

    g1 = col(g, XOR_Z[1])
    b_in = col(b_other, SWAP_Y)
    x_own = row(b_own, SWAP_X)
    g3_mid = col(after(g, b_other), MIDDLE)
    pieces, g1, g3_mid, x_own, b_in, b_own = hold((pieces, g1, g3_mid, x_own, b_in, b_own))

    x_in = row(b_in, SWAP_X)
    a_in = col(after(a_even, b_in), SWAP_Y)
    swapped = [row(b, SWAP_CORE) for b in (b_own, x_own, b_in, pieces[0])]
    pieces, swapped = hold((pieces, swapped))
    got = [col(pieces[d], XOR_Z[d]) for d in (3, 2, 1)]
    piece_x = row(pieces[0], SWAP_X)
    x_in, got, a_in, piece_x = hold((x_in, got, a_in, piece_x))

    swapped += [row(x_in, SWAP_CORE), row(piece_x, SWAP_CORE)]
    a_in, got, swapped = hold((a_in, got, swapped))
    b_rows = [[b_own, x_own, swapped[0], swapped[1]], [b_in, x_in, swapped[2], swapped[4]]]
    piece_rows = [b[None] for b in (pieces[0], piece_x, swapped[3], swapped[5])]

    (p3,) = parts(place, [a_even, a_in], b_rows, [3])
    wire3 = (p3 * WIRE).astype(F16)

    wire3, g1, g3_mid, got = hold((wire3, g1, g3_mid, got))
    got = jnp.stack([got[2], got[1], got[0]])
    i3 = col(wire3, INWARD)
    g2_end = col(g3_mid, OUTWARD)
    g2_mid = col(g1, MIDDLE)
    got_x = row(got, SWAP_X)
    p2, p1, p0 = parts(place, [after(a_even, wire3), a_in], b_rows, [2, 1, 0])
    wire2 = (p2 * WIRE).astype(F16)
    i2 = col(wire2, INWARD)
    turn2 = ((p2 + from_wire(i3)) * WIRE).astype(F16)
    turn2, p1, g2_mid, got_x, g2_end = hold((turn2, p1, g2_mid, got_x, g2_end))


    m2 = col(turn2, MIDDLE)
    g3_end = col(g2_mid, OUTWARD)
    got_rows = [got, got_x, row(got, SWAP_CORE), row(got_x, SWAP_CORE)]

    terms = [((g,), piece_rows, 0)]
    terms += [(left, got_rows, n) for n, left in enumerate([(g1,), (g2_mid, g2_end), (g3_mid, g3_end)])]
    turn3 = ((p3 + from_wire(i2)) * WIRE).astype(F16)
    turn1 = ((p1 + from_wire(m2)) * WIRE).astype(F16)
    turn3, turn1, g3_end = hold((turn3, turn1, g3_end))

    s1 = col(turn1, XOR_Z[1])
    m3 = col(turn3, MIDDLE)
    terms[3] = ((g3_mid, g3_end), got_rows, 2)
    q = to_wire(column(place, terms, 1), SWAP_Y)
    odd = column(place, terms, 0) + from_wire(q)
    even, m3, odd = hold((p0 + from_wire(s1), m3, odd))
    even = even + from_wire(m3)

    result = residual_in.reshape(irreps, row_blocks * block * 2, block)
    done = add_all(place, result, even, odd)
    return done.reshape(residual_in.shape)


def solution(mesh):
    placed = (
        P("row", "col", None, None, None),
        P(None, "row", None, "col", None),
        P(None, "row", None, "col", None),
    )

    def per_device(amp_ladder, integrals, residual_in):
        fits = mesh.shape["row"] == 4 and mesh.shape["col"] == 8
        fits = fits and amp_ladder.shape[0] == 2 and residual_in.shape[3] == 2 and amp_ladder.shape[1] == 2
        return (mixed if fits else gathered)(amp_ladder, integrals, residual_in)

    return jax.shard_map(
        per_device,
        mesh=mesh,
        in_specs=placed,
        out_specs=P(None, "row", None, "col", None),
        check_vma=False,
    )
```

```python
import jax
import jax.numpy as jnp
from jax import lax
from jax.experimental import pallas as pl
from jax.experimental.pallas import tpu as pltpu
from jax.sharding import PartitionSpec as P

BF16, F16, F32 = jnp.bfloat16, jnp.float16, jnp.float32
WIRE = 32.0
PARAMS = pltpu.CompilerParams(vmem_limit_bytes=32 * 2**20)


def gathered(amp_ladder, integrals, residual_in):
    irreps, row_blocks, block = integrals.shape[:3]
    moved = lax.all_to_all(amp_ladder, "col", split_axis=3, concat_axis=1, tiled=True)
    right = lax.all_gather(moved, "row", axis=0, tiled=True)
    left = lax.all_gather(integrals, "col", axis=3, tiled=True)
    inner = left.shape[3] * block
    columns = right.shape[3]
    left = left.reshape(irreps, row_blocks * block, inner)
    right = right.reshape(irreps, inner, columns * block)
    cycle = jnp.einsum("hik,hkj->hij", left, right, preferred_element_type=F32)
    return residual_in + cycle.reshape(irreps, row_blocks, block, columns, block)


def along_z(pairs):
    return [(2 * a + y, 2 * b + y) for a, b in pairs for y in range(2)]


SWAP_Y = [(c, c ^ 1) for c in range(8)]
SWAP_CORE = [(r, r ^ 1) for r in range(4)]
SWAP_X = [(r, r ^ 2) for r in range(4)]
XOR_Z = {d: along_z([(z, z ^ d) for z in range(4)]) for d in (1, 2, 3)}
MIDDLE = along_z([(1, 2), (2, 1)])
INWARD = along_z([(0, 1), (3, 2)])
OUTWARD = along_z([(1, 0), (2, 3)])


def col(x, pairs):
    return lax.ppermute(x, "col", pairs)


def row(x, pairs):
    return lax.ppermute(x, "row", pairs)


def to_wire(x, pairs):
    return col((x * WIRE).astype(F16), pairs)


def from_wire(x):
    return x.astype(F32) * (1 / WIRE)


def after(x, *others):
    return lax.optimization_barrier((x, *others))[0]


def call(body, place, grid, ins, outs, shapes, operands, scratch=(), **more):
    return pl.pallas_call(
        body,
        grid_spec=pltpu.PrefetchScalarGridSpec(
            num_scalar_prefetch=1, grid=grid, in_specs=ins, out_specs=outs, scratch_shapes=list(scratch)
        ),
        out_shape=shapes,
        compiler_params=PARAMS,
        cost_estimate=pl.CostEstimate(flops=0, bytes_accessed=0, transcendentals=0),
        **more,
    )(place, *operands)


def split_rows(place, pairs):
    irreps, double, lanes = pairs.shape
    rows = double // 2

    def body(_, in_ref, even_ref, odd_ref, wide):
        for n, out in enumerate((even_ref, odd_ref)):
            wide[...] = in_ref[n].astype(F32)
            for b in range(2):
                out[0, :, b * lanes : (b + 1) * lanes] = wide[pl.ds(b, rows, stride=2), :].astype(BF16)

    shape = jax.ShapeDtypeStruct((irreps // 2, rows, 2 * lanes), BF16)
    spec = pl.BlockSpec((1, rows, 2 * lanes), lambda i, _: (i, 0, 0))
    return call(
        body, place, (irreps // 2,),
        [pl.BlockSpec((2, double, lanes), lambda i, _: (i, 0, 0))],
        [spec, spec], [shape, shape], [pairs], [pltpu.VMEM((double, lanes), F32)],
    )


def pick_columns(place, amps, irrep, tables):
    _, k_blocks, block, columns, lanes = amps.shape
    sizes = [len(t) for t in tables([0, 0, 0])]

    def body(place_ref, in_ref, *refs):
        outs, wide = refs[:-1], refs[-1]
        wide[...] = in_ref[0, 0].astype(F32).reshape(wide.shape)
        for out, table in zip(outs, tables(place_ref)):
            for n, pair in enumerate(table):
                for b, j in enumerate(pair):
                    out[n, :, b * lanes : (b + 1) * lanes] = wide[pl.ds(j, block, stride=columns), :].astype(BF16)

    return call(
        body, place, (k_blocks,),
        [pl.BlockSpec((1, 1, block, columns, lanes), lambda k, _: (irrep, k, 0, 0, 0))],
        [pl.BlockSpec((n, block, 2 * lanes), lambda k, _: (0, k, 0)) for n in sizes],
        [jax.ShapeDtypeStruct((n, k_blocks * block, 2 * lanes), BF16) for n in sizes],
        [amps], [pltpu.VMEM((block * columns, lanes), F32)],
    )


def parts(place, lefts, rights, steps):
    irreps, rows, kk = lefts[0].shape
    wide = rights[0][0].shape[-1]
    flat = [b for source in rights for b in source]

    def body(place_ref, *refs):
        a_refs, refs = refs[: len(lefts)], refs[len(lefts) :]
        b_refs, outs = refs[: len(flat) * len(steps)], refs[len(flat) * len(steps) :]
        for m in range(4):

            @pl.when(pl.program_id(0) == m)
            def _():
                for n, out in enumerate(outs):
                    total = None
                    for s, a in enumerate(a_refs):
                        b = b_refs[n * len(flat) + 4 * s + m]
                        term = jnp.dot(a[0], b[0], preferred_element_type=F32)
                        total = term if total is None else total + term
                    out[0] = total

    irrep_of = lambda m, p: (p[0] ^ (((m & 1) << 1) | (m >> 1)), 0, 0)
    return call(
        body, place, (irreps,),
        [pl.BlockSpec((1, rows, kk), irrep_of)] * len(lefts)
        + [pl.BlockSpec((1, kk, wide), lambda m, p, d=d: (p[1] ^ d, 0, 0)) for d in steps for _ in flat],
        [pl.BlockSpec((1, rows, wide), irrep_of)] * len(steps),
        [jax.ShapeDtypeStruct((irreps, rows, wide), F32)] * len(steps),
        [*lefts, *(flat * len(steps))],
    )


def column(place, terms, other, start=None):
    irreps, rows, kk = terms[0][0][0].shape
    wide = terms[0][1][0].shape[-1]
    lefts = [left for t in terms for left in t[0]]
    flat = [b for t in terms for b in t[1]]
    given = [] if start is None else [start]

    def body(place_ref, *refs):
        a_refs, b_refs, out = refs[: len(lefts)], refs[len(lefts) : len(lefts) + len(flat)], refs[-1]
        for m in range(4):

            @pl.when(pl.program_id(0) == m)
            def _():
                total = refs[-2][0] if given else None
                at = 0
                for s, t in enumerate(terms):
                    left = a_refs[at][0]
                    if len(t[0]) == 2:
                        left = left + a_refs[at + 1][0]
                    at += len(t[0])
                    term = jnp.dot(left, b_refs[4 * s + m][0, 0], preferred_element_type=F32)
                    total = term if total is None else total + term
                out[0] = total

    irrep_of = lambda m, p: (p[0] ^ (((m & 1) << 1) | (m >> 1)), 0, 0)
    sums = pl.BlockSpec((1, rows, wide), irrep_of)
    return call(
        body, place, (irreps,),
        [pl.BlockSpec((1, rows, kk), irrep_of)] * len(lefts)
        + [pl.BlockSpec((1, 1, kk, wide), lambda m, p, n=t[2]: (n, p[2] ^ other, 0, 0)) for t in terms for _ in range(4)]
        + [sums] * len(given),
        sums,
        jax.ShapeDtypeStruct((irreps, rows, wide), F32),
        [*lefts, *flat, *given],
    )


def add_half(place, residual, cycle, parity, result=None):
    irreps, double, lanes = residual.shape
    rows = double // 2

    def body(_, res_ref, add_ref, *refs):
        out = refs[-1]
        for b in range(2):
            place = pl.ds(b, rows, stride=2)
            out[0, place, :] = res_ref[0, place, :] + add_ref[0, :, b * lanes : (b + 1) * lanes]

    mine = pl.BlockSpec((1, double, lanes), lambda i, _: (2 * i + parity, 0, 0))
    given = [] if result is None else [result]
    return call(
        body, place, (irreps // 2,),
        [mine, pl.BlockSpec((1, rows, 2 * lanes), lambda i, _: (i, 0, 0))] + [pl.BlockSpec(memory_space=pl.ANY)] * len(given),
        mine,
        jax.ShapeDtypeStruct(residual.shape, F32),
        [residual, cycle, *given],
        input_output_aliases={3: 0} if given else {},
    )


def mixed(amp_ladder, integrals, residual_in):
    irreps, row_blocks, block, k_blocks, _ = integrals.shape
    r, c = lax.axis_index("row"), lax.axis_index("col")
    z, y = c // 2, c % 2
    middle = (z == 1) | (z == 2)
    place = jnp.stack([r, z, y]).astype(jnp.int32)

    a_even, g = split_rows(place, integrals.reshape(irreps, row_blocks * block * k_blocks, block))
    amp_ladder = after(amp_ladder, g)
    tables = lambda p: [[[4 * t + 2 * w + b for b in range(2)] for t in range(4)] for w in (p[2], 1 - p[2])]
    b_own, b_other = pick_columns(place, amp_ladder, 0, tables)
    tables = lambda p: [[[4 * (p[1] ^ d) + 2 * w + b for b in range(2)] for w in range(2)] for d in range(4)]
    pieces = pick_columns(place, amp_ladder, 1, tables)

    hold = lax.optimization_barrier

    g1 = col(g, XOR_Z[1])
    b_in = col(b_other, SWAP_Y)
    x_own = row(b_own, SWAP_X)
    g3_mid = col(after(g, b_other), MIDDLE)
    pieces, g1, g3_mid, x_own, b_in, b_own = hold((pieces, g1, g3_mid, x_own, b_in, b_own))

    x_in = row(b_in, SWAP_X)
    a_in = col(a_even, SWAP_Y)
    swapped = [row(b, SWAP_CORE) for b in (b_own, x_own)]
    pieces, swapped = hold((pieces, swapped))
    got = [col(pieces[d], XOR_Z[d]) for d in (3, 2, 1)]
    piece_x = row(pieces[0], SWAP_X)
    x_in, got, a_in, piece_x = hold((x_in, got, a_in, piece_x))
    swapped += [row(b, SWAP_CORE) for b in (b_in, pieces[0], x_in, piece_x)]
    a_in, got, swapped = hold((a_in, got, swapped))
    b_rows = [[b_own, x_own, swapped[0], swapped[1]], [b_in, x_in, swapped[2], swapped[4]]]
    piece_rows = [b[None] for b in (pieces[0], piece_x, swapped[3], swapped[5])]

    (p3,) = parts(place, [a_even, a_in], b_rows, [3])
    wire3 = (p3 * WIRE).astype(F16)
    wire3, g1, g3_mid, got = hold((wire3, g1, g3_mid, got))
    got = jnp.stack([got[2], got[1], got[0]])
    i3 = col(wire3, INWARD)
    g2_end = col(g3_mid, OUTWARD)
    g2_mid = col(g1, MIDDLE)
    got_x = row(got, SWAP_X)
    p2, p1, p0 = parts(place, [after(a_even, wire3), a_in], b_rows, [2, 1, 0])
    wire2 = (p2 * WIRE).astype(F16)
    i2 = col(wire2, INWARD)
    turn2 = ((p2 + from_wire(i3)) * WIRE).astype(F16)
    turn2, p1, g2_mid, got_x, g2_end = hold((turn2, p1, g2_mid, got_x, g2_end))

    m2 = col(turn2, MIDDLE)
    g3_end = col(g2_mid, OUTWARD)
    got_rows = [got, got_x, row(got, SWAP_CORE), row(got_x, SWAP_CORE)]
    terms = [((g,), piece_rows, 0)]
    terms += [(left, got_rows, n) for n, left in enumerate([(g1,), (g2_mid, g2_end), (g3_mid, g3_end)])]
    turn3 = ((p3 + from_wire(i2)) * WIRE).astype(F16)
    turn1 = ((p1 + from_wire(m2)) * WIRE).astype(F16)
    turn3, turn1 = hold((turn3, turn1))
    g3_end = after(g3_end, turn1, turn3)

    s1 = col(turn1, XOR_Z[1])
    m3 = col(turn3, MIDDLE)
    terms[3] = ((g3_mid, g3_end), got_rows, 2)
    q = to_wire(column(place, terms, 1), SWAP_Y)
    own = column(place, terms, 0)
    even = (p0 + from_wire(s1)) + from_wire(m3)
    result = residual_in.reshape(irreps, row_blocks * block * 2, block)
    done = add_half(place, result, even, 0)
    done = add_half(place, result, own + from_wire(q), 1, done)
    return done.reshape(residual_in.shape)


def solution(mesh):
    placed = (
        P("row", "col", None, None, None),
        P(None, "row", None, "col", None),
        P(None, "row", None, "col", None),
    )

    def per_device(amp_ladder, integrals, residual_in):
        fits = mesh.shape["row"] == 4 and mesh.shape["col"] == 8
        fits = fits and amp_ladder.shape[0] == 2 and residual_in.shape[3] == 2 and amp_ladder.shape[1] == 2
        return (mixed if fits else gathered)(amp_ladder, integrals, residual_in)

    return jax.shard_map(
        per_device,
        mesh=mesh,
        in_specs=placed,
        out_specs=P(None, "row", None, "col", None),
        check_vma=False,
    )
```

```python
import jax
import jax.numpy as jnp
from jax import lax
from jax.experimental import pallas as pl
from jax.experimental.pallas import tpu as pltpu
from jax.sharding import PartitionSpec as P

BF16, F16, F32 = jnp.bfloat16, jnp.float16, jnp.float32
WIRE = 32.0
PARAMS = pltpu.CompilerParams(vmem_limit_bytes=32 * 2**20)


def gathered(amp_ladder, integrals, residual_in):
    irreps, row_blocks, block = integrals.shape[:3]
    moved = lax.all_to_all(amp_ladder, "col", split_axis=3, concat_axis=1, tiled=True)
    right = lax.all_gather(moved, "row", axis=0, tiled=True)
    left = lax.all_gather(integrals, "col", axis=3, tiled=True)
    inner = left.shape[3] * block
    columns = right.shape[3]
    left = left.reshape(irreps, row_blocks * block, inner)
    right = right.reshape(irreps, inner, columns * block)
    cycle = jnp.einsum("hik,hkj->hij", left, right, preferred_element_type=F32)
    return residual_in + cycle.reshape(irreps, row_blocks, block, columns, block)


def along_z(pairs):
    return [(2 * a + y, 2 * b + y) for a, b in pairs for y in range(2)]


SWAP_Y = [(c, c ^ 1) for c in range(8)]
SWAP_CORE = [(r, r ^ 1) for r in range(4)]
SWAP_X = [(r, r ^ 2) for r in range(4)]
XOR_Z = {d: along_z([(z, z ^ d) for z in range(4)]) for d in (1, 2, 3)}
MIDDLE = along_z([(1, 2), (2, 1)])
INWARD = along_z([(0, 1), (3, 2)])
OUTWARD = along_z([(1, 0), (2, 3)])


def col(x, pairs):
    return lax.ppermute(x, "col", pairs)


def row(x, pairs):
    return lax.ppermute(x, "row", pairs)


def to_wire(x, pairs):
    return col((x * WIRE).astype(F16), pairs)


def from_wire(x):
    return x.astype(F32) * (1 / WIRE)


def after(x, *others):
    return lax.optimization_barrier((x, *others))[0]


def call(body, place, grid, ins, outs, shapes, operands, scratch=(), **more):
    return pl.pallas_call(
        body,
        grid_spec=pltpu.PrefetchScalarGridSpec(
            num_scalar_prefetch=1, grid=grid, in_specs=ins, out_specs=outs, scratch_shapes=list(scratch)
        ),
        out_shape=shapes,
        compiler_params=PARAMS,
        cost_estimate=pl.CostEstimate(flops=0, bytes_accessed=0, transcendentals=0),
        **more,
    )(place, *operands)


def split_rows(place, pairs):
    irreps, double, lanes = pairs.shape
    rows = double // 2

    def body(_, in_ref, even_ref, odd_ref, wide):
        for n, out in enumerate((even_ref, odd_ref)):
            wide[...] = in_ref[n].astype(F32)
            for b in range(2):
                out[0, :, b * lanes : (b + 1) * lanes] = wide[pl.ds(b, rows, stride=2), :].astype(BF16)

    shape = jax.ShapeDtypeStruct((irreps // 2, rows, 2 * lanes), BF16)
    spec = pl.BlockSpec((1, rows, 2 * lanes), lambda i, _: (i, 0, 0))
    return call(
        body, place, (irreps // 2,),
        [pl.BlockSpec((2, double, lanes), lambda i, _: (i, 0, 0))],
        [spec, spec], [shape, shape], [pairs], [pltpu.VMEM((double, lanes), F32)],
    )


def pick_columns(place, amps, irrep, tables):
    _, k_blocks, block, columns, lanes = amps.shape
    sizes = [len(t) for t in tables([0, 0, 0])]

    def body(place_ref, in_ref, *refs):
        outs, wide = refs[:-1], refs[-1]
        wide[...] = in_ref[0, 0].astype(F32).reshape(wide.shape)
        for out, table in zip(outs, tables(place_ref)):
            for n, pair in enumerate(table):
                for b, j in enumerate(pair):
                    out[n, :, b * lanes : (b + 1) * lanes] = wide[pl.ds(j, block, stride=columns), :].astype(BF16)

    return call(
        body, place, (k_blocks,),
        [pl.BlockSpec((1, 1, block, columns, lanes), lambda k, _: (irrep, k, 0, 0, 0))],
        [pl.BlockSpec((n, block, 2 * lanes), lambda k, _: (0, k, 0)) for n in sizes],
        [jax.ShapeDtypeStruct((n, k_blocks * block, 2 * lanes), BF16) for n in sizes],
        [amps], [pltpu.VMEM((block * columns, lanes), F32)],
    )


def parts(place, lefts, rights, steps):
    irreps, rows, kk = lefts[0].shape
    wide = rights[0][0].shape[-1]
    flat = [b for source in rights for b in source]

    def body(place_ref, *refs):
        a_refs, refs = refs[: len(lefts)], refs[len(lefts) :]
        b_refs, outs = refs[: len(flat) * len(steps)], refs[len(flat) * len(steps) :]
        for m in range(4):

            @pl.when(pl.program_id(0) == m)
            def _():
                for n, out in enumerate(outs):
                    total = None
                    for s, a in enumerate(a_refs):
                        b = b_refs[n * len(flat) + 4 * s + m]
                        term = jnp.dot(a[0], b[0], preferred_element_type=F32)
                        total = term if total is None else total + term
                    out[0] = total

    irrep_of = lambda m, p: (p[0] ^ (((m & 1) << 1) | (m >> 1)), 0, 0)
    return call(
        body, place, (irreps,),
        [pl.BlockSpec((1, rows, kk), irrep_of)] * len(lefts)
        + [pl.BlockSpec((1, kk, wide), lambda m, p, d=d: (p[1] ^ d, 0, 0)) for d in steps for _ in flat],
        [pl.BlockSpec((1, rows, wide), irrep_of)] * len(steps),
        [jax.ShapeDtypeStruct((irreps, rows, wide), F32)] * len(steps),
        [*lefts, *(flat * len(steps))],
    )


def column(place, terms, other, start=None):
    irreps, rows, kk = terms[0][0][0].shape
    wide = terms[0][1][0].shape[-1]
    lefts = [left for t in terms for left in t[0]]
    flat = [b for t in terms for b in t[1]]
    given = [] if start is None else [start]

    def body(place_ref, *refs):
        a_refs, b_refs, out = refs[: len(lefts)], refs[len(lefts) : len(lefts) + len(flat)], refs[-1]
        for m in range(4):

            @pl.when(pl.program_id(0) == m)
            def _():
                total = refs[-2][0] if given else None
                at = 0
                for s, t in enumerate(terms):
                    left = a_refs[at][0]
                    if len(t[0]) == 2:
                        left = left + a_refs[at + 1][0]
                    at += len(t[0])
                    term = jnp.dot(left, b_refs[4 * s + m][0, 0], preferred_element_type=F32)
                    total = term if total is None else total + term
                out[0] = total

    irrep_of = lambda m, p: (p[0] ^ (((m & 1) << 1) | (m >> 1)), 0, 0)
    sums = pl.BlockSpec((1, rows, wide), irrep_of)
    return call(
        body, place, (irreps,),
        [pl.BlockSpec((1, rows, kk), irrep_of)] * len(lefts)
        + [pl.BlockSpec((1, 1, kk, wide), lambda m, p, n=t[2]: (n, p[2] ^ other, 0, 0)) for t in terms for _ in range(4)]
        + [sums] * len(given),
        sums,
        jax.ShapeDtypeStruct((irreps, rows, wide), F32),
        [*lefts, *flat, *given],
    )


def add_half(place, residual, cycle, parity, result=None):
    irreps, double, lanes = residual.shape
    rows = double // 2

    def body(_, res_ref, add_ref, *refs):
        out = refs[-1]
        for b in range(2):
            place = pl.ds(b, rows, stride=2)
            out[0, place, :] = res_ref[0, place, :] + add_ref[0, :, b * lanes : (b + 1) * lanes]

    mine = pl.BlockSpec((1, double, lanes), lambda i, _: (2 * i + parity, 0, 0))
    given = [] if result is None else [result]
    return call(
        body, place, (irreps // 2,),
        [mine, pl.BlockSpec((1, rows, 2 * lanes), lambda i, _: (i, 0, 0))] + [pl.BlockSpec(memory_space=pl.ANY)] * len(given),
        mine,
        jax.ShapeDtypeStruct(residual.shape, F32),
        [residual, cycle, *given],
        input_output_aliases={3: 0} if given else {},
    )


def mixed(amp_ladder, integrals, residual_in):
    irreps, row_blocks, block, k_blocks, _ = integrals.shape
    r, c = lax.axis_index("row"), lax.axis_index("col")
    z, y = c // 2, c % 2
    middle = (z == 1) | (z == 2)
    place = jnp.stack([r, z, y]).astype(jnp.int32)

    a_even, g = split_rows(place, integrals.reshape(irreps, row_blocks * block * k_blocks, block))
    amp_ladder = after(amp_ladder, g)
    tables = lambda p: [[[4 * t + 2 * w + b for b in range(2)] for t in range(4)] for w in (p[2], 1 - p[2])]
    b_own, b_other = pick_columns(place, amp_ladder, 0, tables)
    tables = lambda p: [[[4 * (p[1] ^ d) + 2 * w + b for b in range(2)] for w in range(2)] for d in range(4)]
    pieces = pick_columns(place, amp_ladder, 1, tables)

    hold = lax.optimization_barrier

    g1 = col(g, XOR_Z[1])
    b_in = col(b_other, SWAP_Y)
    x_own = row(b_own, SWAP_X)
    g3_mid = col(after(g, b_other), MIDDLE)
    pieces, g1, g3_mid, x_own, b_in, b_own = hold((pieces, g1, g3_mid, x_own, b_in, b_own))

    x_in = row(b_in, SWAP_X)
    a_in = col(a_even, SWAP_Y)
    swapped = [row(b, SWAP_CORE) for b in (b_own, x_own)]
    pieces, swapped = hold((pieces, swapped))
    got = [col(pieces[d], XOR_Z[d]) for d in (3, 1, 2)]
    piece_x = row(pieces[0], SWAP_X)
    x_in, got, a_in, piece_x = hold((x_in, got, a_in, piece_x))
    swapped += [row(b, SWAP_CORE) for b in (b_in, pieces[0], x_in, piece_x)]
    a_in, got, swapped = hold((a_in, got, swapped))
    b_rows = [[b_own, x_own, swapped[0], swapped[1]], [b_in, x_in, swapped[2], swapped[4]]]
    piece_rows = [b[None] for b in (pieces[0], piece_x, swapped[3], swapped[5])]

    (p3,) = parts(place, [a_even, a_in], b_rows, [3])
    wire3 = (p3 * WIRE).astype(F16)
    wire3, g1, g3_mid, got = hold((wire3, g1, g3_mid, got))
    got = jnp.stack([got[1], got[2], got[0]])
    i3 = col(wire3, INWARD)
    g2_end = col(g3_mid, OUTWARD)
    g2_mid = col(g1, MIDDLE)
    got_x = row(got, SWAP_X)
    p2, p1, p0 = parts(place, [after(a_even, wire3), a_in], b_rows, [2, 1, 0])
    wire2 = (p2 * WIRE).astype(F16)
    i2 = col(wire2, INWARD)
    turn2 = ((p2 + from_wire(i3)) * WIRE).astype(F16)
    turn2, p1, g2_mid, got_x, g2_end = hold((turn2, p1, g2_mid, got_x, g2_end))

    m2 = col(turn2, MIDDLE)
    g3_end = col(g2_mid, OUTWARD)
    got_rows = [got, got_x, row(got, SWAP_CORE), row(got_x, SWAP_CORE)]
    terms = [((g,), piece_rows, 0)]
    terms += [(left, got_rows, n) for n, left in enumerate([(g1,), (g2_mid, g2_end), (g3_mid, g3_end)])]
    turn3 = ((p3 + from_wire(i2)) * WIRE).astype(F16)
    turn1 = ((p1 + from_wire(m2)) * WIRE).astype(F16)
    turn3, turn1 = hold((turn3, turn1))
    g3_end = after(g3_end, turn1, turn3)

    s1 = col(turn1, XOR_Z[1])
    m3 = col(turn3, MIDDLE)
    terms[3] = ((g3_mid, g3_end), got_rows, 2)
    q = to_wire(column(place, terms, 1), SWAP_Y)
    own = column(place, terms, 0)
    even = (p0 + from_wire(s1)) + from_wire(m3)
    result = residual_in.reshape(irreps, row_blocks * block * 2, block)
    done = add_half(place, result, even, 0)
    done = add_half(place, result, own + from_wire(q), 1, done)
    return done.reshape(residual_in.shape)


def solution(mesh):
    placed = (
        P("row", "col", None, None, None),
        P(None, "row", None, "col", None),
        P(None, "row", None, "col", None),
    )

    def per_device(amp_ladder, integrals, residual_in):
        fits = mesh.shape["row"] == 4 and mesh.shape["col"] == 8
        fits = fits and amp_ladder.shape[0] == 2 and residual_in.shape[3] == 2 and amp_ladder.shape[1] == 2
        return (mixed if fits else gathered)(amp_ladder, integrals, residual_in)

    return jax.shard_map(
        per_device,
        mesh=mesh,
        in_specs=placed,
        out_specs=P(None, "row", None, "col", None),
        check_vma=False,
    )
```

```python
import jax
import jax.numpy as jnp
from jax import lax
from jax.experimental import pallas as pl
from jax.experimental.pallas import tpu as pltpu
from jax.sharding import PartitionSpec as P

BF16, F16, F32 = jnp.bfloat16, jnp.float16, jnp.float32
WIRE = 32.0
PARAMS = pltpu.CompilerParams(vmem_limit_bytes=32 * 2**20)


def gathered(amp_ladder, integrals, residual_in):
    irreps, row_blocks, block = integrals.shape[:3]
    moved = lax.all_to_all(amp_ladder, "col", split_axis=3, concat_axis=1, tiled=True)
    right = lax.all_gather(moved, "row", axis=0, tiled=True)
    left = lax.all_gather(integrals, "col", axis=3, tiled=True)
    inner = left.shape[3] * block
    columns = right.shape[3]
    left = left.reshape(irreps, row_blocks * block, inner)
    right = right.reshape(irreps, inner, columns * block)
    cycle = jnp.einsum("hik,hkj->hij", left, right, preferred_element_type=F32)
    return residual_in + cycle.reshape(irreps, row_blocks, block, columns, block)


def along_z(pairs):
    return [(2 * a + y, 2 * b + y) for a, b in pairs for y in range(2)]


SWAP_Y = [(c, c ^ 1) for c in range(8)]
SWAP_CORE = [(r, r ^ 1) for r in range(4)]
SWAP_X = [(r, r ^ 2) for r in range(4)]
XOR_Z = {d: along_z([(z, z ^ d) for z in range(4)]) for d in (1, 2, 3)}
MIDDLE = along_z([(1, 2), (2, 1)])
INWARD = along_z([(0, 1), (3, 2)])
OUTWARD = along_z([(1, 0), (2, 3)])


def col(x, pairs):
    return lax.ppermute(x, "col", pairs)


def row(x, pairs):
    return lax.ppermute(x, "row", pairs)


def to_wire(x, pairs):
    return col((x * WIRE).astype(F16), pairs)


def from_wire(x):
    return x.astype(F32) * (1 / WIRE)


def after(x, *others):
    return lax.optimization_barrier((x, *others))[0]


def call(body, place, grid, ins, outs, shapes, operands, scratch=(), **more):
    return pl.pallas_call(
        body,
        grid_spec=pltpu.PrefetchScalarGridSpec(
            num_scalar_prefetch=1, grid=grid, in_specs=ins, out_specs=outs, scratch_shapes=list(scratch)
        ),
        out_shape=shapes,
        compiler_params=PARAMS,
        cost_estimate=pl.CostEstimate(flops=0, bytes_accessed=0, transcendentals=0),
        **more,
    )(place, *operands)


def split_rows(place, pairs):
    irreps, double, lanes = pairs.shape
    rows = double // 2

    def body(_, in_ref, even_ref, odd_ref, wide):
        for n, out in enumerate((even_ref, odd_ref)):
            wide[...] = in_ref[n].astype(F32)
            for b in range(2):
                out[0, :, b * lanes : (b + 1) * lanes] = wide[pl.ds(b, rows, stride=2), :].astype(BF16)

    shape = jax.ShapeDtypeStruct((irreps // 2, rows, 2 * lanes), BF16)
    spec = pl.BlockSpec((1, rows, 2 * lanes), lambda i, _: (i, 0, 0))
    return call(
        body, place, (irreps // 2,),
        [pl.BlockSpec((2, double, lanes), lambda i, _: (i, 0, 0))],
        [spec, spec], [shape, shape], [pairs], [pltpu.VMEM((double, lanes), F32)],
    )


def pick_columns(place, amps, irrep, tables):
    _, k_blocks, block, columns, lanes = amps.shape
    sizes = [len(t) for t in tables([0, 0, 0])]

    def body(place_ref, in_ref, *refs):
        outs, wide = refs[:-1], refs[-1]
        wide[...] = in_ref[0, 0].astype(F32).reshape(wide.shape)
        for out, table in zip(outs, tables(place_ref)):
            for n, pair in enumerate(table):
                for b, j in enumerate(pair):
                    out[n, :, b * lanes : (b + 1) * lanes] = wide[pl.ds(j, block, stride=columns), :].astype(BF16)

    return call(
        body, place, (k_blocks,),
        [pl.BlockSpec((1, 1, block, columns, lanes), lambda k, _: (irrep, k, 0, 0, 0))],
        [pl.BlockSpec((n, block, 2 * lanes), lambda k, _: (0, k, 0)) for n in sizes],
        [jax.ShapeDtypeStruct((n, k_blocks * block, 2 * lanes), BF16) for n in sizes],
        [amps], [pltpu.VMEM((block * columns, lanes), F32)],
    )


def parts(place, lefts, rights, steps):
    irreps, rows, kk = lefts[0].shape
    wide = rights[0][0].shape[-1]
    flat = [b for source in rights for b in source]

    def body(place_ref, *refs):
        a_refs, refs = refs[: len(lefts)], refs[len(lefts) :]
        b_refs, outs = refs[: len(flat) * len(steps)], refs[len(flat) * len(steps) :]
        for m in range(4):

            @pl.when(pl.program_id(0) == m)
            def _():
                for n, out in enumerate(outs):
                    total = None
                    for s, a in enumerate(a_refs):
                        b = b_refs[n * len(flat) + 4 * s + m]
                        term = jnp.dot(a[0], b[0], preferred_element_type=F32)
                        total = term if total is None else total + term
                    out[0] = total

    irrep_of = lambda m, p: (p[0] ^ (((m & 1) << 1) | (m >> 1)), 0, 0)
    return call(
        body, place, (irreps,),
        [pl.BlockSpec((1, rows, kk), irrep_of)] * len(lefts)
        + [pl.BlockSpec((1, kk, wide), lambda m, p, d=d: (p[1] ^ d, 0, 0)) for d in steps for _ in flat],
        [pl.BlockSpec((1, rows, wide), irrep_of)] * len(steps),
        [jax.ShapeDtypeStruct((irreps, rows, wide), F32)] * len(steps),
        [*lefts, *(flat * len(steps))],
    )


def column(place, terms, other, start=None):
    irreps, rows, kk = terms[0][0][0].shape
    wide = terms[0][1][0].shape[-1]
    lefts = [left for t in terms for left in t[0]]
    flat = [b for t in terms for b in t[1]]
    given = [] if start is None else [start]

    def body(place_ref, *refs):
        a_refs, b_refs, out = refs[: len(lefts)], refs[len(lefts) : len(lefts) + len(flat)], refs[-1]
        for m in range(4):

            @pl.when(pl.program_id(0) == m)
            def _():
                total = refs[-2][0] if given else None
                at = 0
                for s, t in enumerate(terms):
                    left = a_refs[at][0]
                    if len(t[0]) == 2:
                        left = left + a_refs[at + 1][0]
                    at += len(t[0])
                    term = jnp.dot(left, b_refs[4 * s + m][0, 0], preferred_element_type=F32)
                    total = term if total is None else total + term
                out[0] = total

    irrep_of = lambda m, p: (p[0] ^ (((m & 1) << 1) | (m >> 1)), 0, 0)
    sums = pl.BlockSpec((1, rows, wide), irrep_of)
    return call(
        body, place, (irreps,),
        [pl.BlockSpec((1, rows, kk), irrep_of)] * len(lefts)
        + [pl.BlockSpec((1, 1, kk, wide), lambda m, p, n=t[2]: (n, p[2] ^ other, 0, 0)) for t in terms for _ in range(4)]
        + [sums] * len(given),
        sums,
        jax.ShapeDtypeStruct((irreps, rows, wide), F32),
        [*lefts, *flat, *given],
    )


def add_half(place, residual, cycle, parity, result=None):
    irreps, double, lanes = residual.shape
    rows = double // 2

    def body(_, res_ref, add_ref, *refs):
        out = refs[-1]
        for b in range(2):
            place = pl.ds(b, rows, stride=2)
            out[0, place, :] = res_ref[0, place, :] + add_ref[0, :, b * lanes : (b + 1) * lanes]

    mine = pl.BlockSpec((1, double, lanes), lambda i, _: (2 * i + parity, 0, 0))
    given = [] if result is None else [result]
    return call(
        body, place, (irreps // 2,),
        [mine, pl.BlockSpec((1, rows, 2 * lanes), lambda i, _: (i, 0, 0))] + [pl.BlockSpec(memory_space=pl.ANY)] * len(given),
        mine,
        jax.ShapeDtypeStruct(residual.shape, F32),
        [residual, cycle, *given],
        input_output_aliases={3: 0} if given else {},
    )


def mixed(amp_ladder, integrals, residual_in):
    irreps, row_blocks, block, k_blocks, _ = integrals.shape
    r, c = lax.axis_index("row"), lax.axis_index("col")
    z, y = c // 2, c % 2
    middle = (z == 1) | (z == 2)
    place = jnp.stack([r, z, y]).astype(jnp.int32)

    a_even, g = split_rows(place, integrals.reshape(irreps, row_blocks * block * k_blocks, block))
    amp_ladder = after(amp_ladder, g)
    tables = lambda p: [[[4 * t + 2 * w + b for b in range(2)] for t in range(4)] for w in (p[2], 1 - p[2])]
    b_own, b_other = pick_columns(place, amp_ladder, 0, tables)
    tables = lambda p: [[[4 * (p[1] ^ d) + 2 * w + b for b in range(2)] for w in range(2)] for d in range(4)]
    pieces = pick_columns(place, amp_ladder, 1, tables)

    hold = lax.optimization_barrier

    g1 = col(g, XOR_Z[1])
    b_in = col(b_other, SWAP_Y)
    x_own = row(b_own, SWAP_X)
    g3_mid = col(after(g, b_other), MIDDLE)
    pieces, g1, g3_mid, x_own, b_in, b_own = hold((pieces, g1, g3_mid, x_own, b_in, b_own))

    x_in = row(b_in, SWAP_X)
    a_in = col(a_even, SWAP_Y)
    swapped = [row(b, SWAP_CORE) for b in (b_own, x_own)]
    pieces, swapped = hold((pieces, swapped))
    got = [col(pieces[d], XOR_Z[d]) for d in (3, 2, 1)]
    piece_x = row(pieces[0], SWAP_X)
    x_in, got, a_in, piece_x = hold((x_in, got, a_in, piece_x))
    swapped += [row(b, SWAP_CORE) for b in (b_in, x_in)]
    a_in, got, swapped = hold((a_in, got, swapped))
    b_rows = [[b_own, x_own, swapped[0], swapped[1]], [b_in, x_in, swapped[2], swapped[3]]]
    piece_core = [row(after(b, swapped[3]), SWAP_CORE) for b in (pieces[0], piece_x)]

    (p3,) = parts(place, [a_even, a_in], b_rows, [3])
    wire3 = (p3 * WIRE).astype(F16)
    wire3, g1, g3_mid, got, piece_core = hold((wire3, g1, g3_mid, got, piece_core))
    piece_rows = [b[None] for b in (pieces[0], piece_x, *piece_core)]
    got = jnp.stack([got[2], got[1], got[0]])
    i3 = col(wire3, INWARD)
    g2_end = col(g3_mid, OUTWARD)
    g2_mid = col(g1, MIDDLE)
    got_x = row(got, SWAP_X)
    p2, p1, p0 = parts(place, [after(a_even, wire3), a_in], b_rows, [2, 1, 0])
    wire2 = (p2 * WIRE).astype(F16)
    i2 = col(wire2, INWARD)
    turn2 = ((p2 + from_wire(i3)) * WIRE).astype(F16)
    turn2, p1, g2_mid, got_x, g2_end = hold((turn2, p1, g2_mid, got_x, g2_end))

    m2 = col(turn2, MIDDLE)
    g3_end = col(g2_mid, OUTWARD)
    got_rows = [got, got_x, row(got, SWAP_CORE), row(got_x, SWAP_CORE)]
    terms = [((g,), piece_rows, 0)]
    terms += [(left, got_rows, n) for n, left in enumerate([(g1,), (g2_mid, g2_end), (g3_mid, g3_end)])]
    turn3 = ((p3 + from_wire(i2)) * WIRE).astype(F16)
    turn1 = ((p1 + from_wire(m2)) * WIRE).astype(F16)
    turn3, turn1 = hold((turn3, turn1))
    g3_end = after(g3_end, turn1, turn3)

    s1 = col(turn1, XOR_Z[1])
    m3 = col(turn3, MIDDLE)
    terms[3] = ((g3_mid, g3_end), got_rows, 2)
    q = to_wire(column(place, terms, 1), SWAP_Y)
    own = column(place, terms, 0)
    even = (p0 + from_wire(s1)) + from_wire(m3)
    result = residual_in.reshape(irreps, row_blocks * block * 2, block)
    done = add_half(place, result, even, 0)
    done = add_half(place, result, own + from_wire(q), 1, done)
    return done.reshape(residual_in.shape)


def solution(mesh):
    placed = (
        P("row", "col", None, None, None),
        P(None, "row", None, "col", None),
        P(None, "row", None, "col", None),
    )

    def per_device(amp_ladder, integrals, residual_in):
        fits = mesh.shape["row"] == 4 and mesh.shape["col"] == 8
        fits = fits and amp_ladder.shape[0] == 2 and residual_in.shape[3] == 2 and amp_ladder.shape[1] == 2
        return (mixed if fits else gathered)(amp_ladder, integrals, residual_in)

    return jax.shard_map(
        per_device,
        mesh=mesh,
        in_specs=placed,
        out_specs=P(None, "row", None, "col", None),
        check_vma=False,
    )
```
